128 devices in a mesh: seq: 32 (over x, y, core), exp: 4 (over z).
Axes of the slice: x: 4, y: 4, z: 4, core: 2. Of those that a mesh axis runs over, the one named last changes fastest.
Arguments:
- query_heads: bfloat16 [16384, 8192], P('seq', 'exp'), may hold values from -6 to 6
- key_heads: bfloat16 [16384, 8192], P('seq', 'exp'), may hold values from -6 to 6
- value_heads: bfloat16 [16384, 8192], P('seq', 'exp'), may hold values from -6 to 6
- decay_rate: float32 [64, 16384], P('exp', 'seq'), may hold values from 0 to 0.9, as said below
- norm_gain: float32 [8192], P('exp'), may hold values from 0.1 to 1.9
- moe_input: bfloat16 [16384, 3072], P(('seq', 'exp')), may hold values from -6 to 6
- route_ids: int32 [16384, 2], P('seq'), may hold values from 0 to 15, all different within a row; in each aligned block of 128 rows (0 to 127, 128 to 255, ...) at most 18 rows name the same one
- route_gates: float32 [16384, 2], P('seq'), may hold values from 0.2 to 1
- w_gate: bfloat16 [32, 3072, 2304], P('seq', None, 'exp'), may hold values from -0.109375 to 0.109375
- w_up: bfloat16 [32, 3072, 2304], P('seq', None, 'exp'), may hold values from -0.109375 to 0.109375
- w_down: bfloat16 [32, 2304, 3072], P('seq', 'exp'), may hold values from -0.09375 to 0.09375
Outputs:
- attn_out: bfloat16 [16384, 8192], P('seq', 'exp')
- moe_out: bfloat16 [16384, 3072], P(('seq', 'exp'))
The draws below stay inside these ranges and needn't reach their ends.
Inputs may be any that keep to these rules, and one draw needn't show every extreme that they name: `route_ids`: in each aligned block of 128 rows (the rows of one device of moe_input) no expert is named by more than 18 rows, a bound that some block reaches; the two ids of a row differ. `decay_rate`: nonnegative decay rates.
All inputs are finite; a program needn't handle non-finite values.
Results may differ from the reference program's by a relative error of at most 0.017.
Values may be sent and summed in bfloat16 or wider, within the bound.
No kernel may reach another device: no remote copies, remote signals or barrier semaphores. Data moves between devices by JAX's collectives and lax.ppermute only.
A program may use at most 192 MiB of HBM per device.

```python
import math
import jax
import jax.numpy as jnp
import numpy as np
from jax import lax

D = 3072
ATTENTION_COUNT = 64
HD = 128
FF = 4608
BLOCK = 512
EXPERTS = 16
TOKEN_SPAN = 16384
ROWS = 128
FFH = 2304
FFQ = 576
CAP = 18
N_SEQ = 32
N_EXP = 4


def draw_decay_rate(key, part):
    key = jax.random.fold_in(key, 11)
    keys = jax.random.split(key, 7)
    share = 0.5
    slow = jax.random.uniform(keys[0], (ATTENTION_COUNT,)) < share
    slow_rate = jax.random.uniform(keys[1], (ATTENTION_COUNT,), minval=0.02, maxval=0.2) * (math.log(10.0) / TOKEN_SPAN)
    fast_rate = jnp.exp(jax.random.uniform(keys[2], (ATTENTION_COUNT,), minval=math.log(1.0 / 50.0), maxval=math.log(1.0 / 30.0)))
    starting_shift = jnp.where(slow, slow_rate, fast_rate)
    tile_factor = jnp.exp(jax.random.uniform(keys[3], (ATTENTION_COUNT, TOKEN_SPAN // BLOCK), minval=-0.7, maxval=0.7))
    tile_factor = jnp.repeat(tile_factor, BLOCK, axis=1)
    approximate_guess = jnp.exp(jax.random.uniform(keys[4], (ATTENTION_COUNT, TOKEN_SPAN), minval=-0.7, maxval=0.7))
    marker_locations = jax.random.randint(keys[5], (3,), 0, TOKEN_SPAN)
    location_ordinals = jnp.arange(TOKEN_SPAN)
    objective_scores = jax.random.uniform(keys[6], (3, ATTENTION_COUNT), minval=0.22, maxval=0.69)
    cluster_batch = jnp.zeros((ATTENTION_COUNT, TOKEN_SPAN), jnp.float32)
    for integer_quantity in range(3):
        cluster_batch = cluster_batch + (location_ordinals[None, :] == marker_locations[integer_quantity]).astype(jnp.float32) * objective_scores[integer_quantity][:, None]
    return (starting_shift[:, None] * tile_factor * approximate_guess + cluster_batch).astype(jnp.float32)


def shard_levels(rng, dims, shards, smallest, top_value):
    gain, own = 1.0, jax.random.fold_in(rng, 6)
    for position, blocks in shards:
        draws = jnp.exp(jax.random.uniform(jax.random.fold_in(own, position), (blocks,), jnp.float32, smallest / len(shards), top_value / len(shards)))
        gain = gain * jnp.repeat(draws, dims[position] // blocks).reshape([-1 if axis == position else 1 for axis in range(len(dims))])
    return gain


def assign_block(stream_key, own, number, rows, amount, top, limit, lean):
    ranking = jax.random.permutation(stream_key, amount)
    crowded, usual = load_shares(amount, rows * top, limit, lean, True), load_shares(amount, rows * top, limit, lean, False)
    places = jnp.arange(amount)

    def named(sizes, offset_by):
        used = int((sizes > 0).sum())
        fixed = max(1, used // 4)
        moved = fixed + (places - fixed + offset_by * (used - fixed)) % max(1, amount - fixed)
        return jnp.zeros((amount,), jnp.int32).at[ranking[jnp.where(places < fixed, places, moved)]].set(jnp.asarray(sizes, jnp.int32))

    sizes = jnp.where(number % 4 == 0, named(crowded, number // 4), named(usual, number - number // 4 - 1))
    mixed = jax.random.permutation(jax.random.fold_in(own, 3), amount)
    donor, sink = mixed[0:amount // 2 * 2:2], mixed[1:amount // 2 * 2:2]
    room = jnp.minimum(sizes[donor] - 1, limit - sizes[sink]) // 2
    room = jnp.where((donor == ranking[0]) | (sink == ranking[0]) | (sizes[sink] == 0), 0, jnp.maximum(room, 0))
    moved = jax.random.randint(jax.random.fold_in(own, 4), (amount // 2,), 0, 1 << 20) % (room + 1)
    sizes = sizes.at[donor].add(-moved).at[sink].add(moved)
    members = jnp.searchsorted(jnp.cumsum(sizes), jnp.arange(rows * top), side="right").astype(jnp.int32)
    listing = members.reshape(top, rows).T
    listing = listing[jax.random.permutation(jax.random.fold_in(own, 1), rows)]
    offset_by = jax.random.randint(jax.random.fold_in(own, 2), (rows, 1), 0, top)
    return jnp.take_along_axis(listing, (jnp.arange(top)[None, :] + offset_by) % top, axis=1)


def load_shares(count, total, limit, lean, full):
    loads = [(1 << 20) // math.isqrt(rank ** lean) + 1 for rank in range(1, count + 1)]
    largest = limit if full else min(limit, max(-(-total // count), total * loads[0] // sum(loads)))
    least = 1 if total - largest >= count - 1 else 0
    given, surplus = [largest] + [least] * (count - 1), total - largest - least * (count - 1)
    while surplus > 0:
        free = [i for i in range(1, count) if given[i] < largest] or [i for i in range(1, count) if given[i] < limit]
        whole, budget = sum([loads[i] for i in free]), surplus
        for i in free:
            more = min(limit - given[i], max(1, budget * loads[i] // whole), surplus)
            given[i] = given[i] + more
            surplus = surplus - more
    return np.array(given)


def scatter_about(rng, shape, scale, bound, cuts=(), kind=jnp.bfloat16):
    gain = shard_levels(rng, shape, cuts, -0.22, 0.18) if cuts else 1.0
    result = jax.random.normal(rng, shape, jnp.float32) * scale * gain
    return jnp.minimum(jnp.maximum(result, -bound), bound).astype(kind)


def setup_inputs(seed: int = 0) -> dict:
    key_list = jax.random.split(jax.random.key(seed), 12)
    query_heads = scatter_about(key_list[0], (TOKEN_SPAN, ATTENTION_COUNT * HD), 1.0, 6.0, ((0, 32), (1, 4)))
    key_heads = scatter_about(key_list[1], (TOKEN_SPAN, ATTENTION_COUNT * HD), 1.0, 6.0, ((0, 32), (1, 4)))
    value_heads = scatter_about(key_list[2], (TOKEN_SPAN, ATTENTION_COUNT * HD), 1.0, 6.0, ((0, 32), (1, 4)))
    decay_rate = draw_decay_rate(jax.random.fold_in(key_list[11], 71), 0)
    norm_gain = jnp.clip(1.0 + 0.18 * jax.random.normal(key_list[4], (ATTENTION_COUNT * HD,), jnp.float32), 0.1, 1.9)
    moe_input = scatter_about(key_list[5], (TOKEN_SPAN, D), 1.0, 6.0, ((0, 128),))
    route_ids_keys = jax.random.split(jax.random.fold_in(key_list[6], 1), TOKEN_SPAN // ROWS)
    route_ids_turns = jax.random.permutation(jax.random.fold_in(key_list[6], 3), TOKEN_SPAN // ROWS)
    route_ids = jax.vmap(lambda own, number: assign_block(jax.random.fold_in(key_list[6], 2), own, number, ROWS, EXPERTS, 2, CAP, 2))(route_ids_keys, route_ids_turns).reshape((TOKEN_SPAN, 2))
    route_gates = jnp.clip(0.2 + 0.8 * jax.random.uniform(key_list[7], (TOKEN_SPAN, 2), jnp.float32) ** shard_levels(key_list[7], (TOKEN_SPAN, 2), ((0, 32),), -0.2, 0.2), 0.2, 1.0)
    w_gate = scatter_about(key_list[8], (N_SEQ, D, FFH), D ** -0.5, 0.109375, ((0, 32), (2, 4)))
    w_up = scatter_about(key_list[9], (N_SEQ, D, FFH), D ** -0.5, 0.109375, ((0, 32), (2, 4)))
    w_down = scatter_about(key_list[10], (N_SEQ, FFH, D), FF ** -0.5, 0.09375, ((0, 32), (1, 4)))
    return {"query_heads": query_heads, "key_heads": key_heads, "value_heads": value_heads, "decay_rate": decay_rate, "norm_gain": norm_gain, "moe_input": moe_input, "route_ids": route_ids, "route_gates": route_gates, "w_gate": w_gate, "w_up": w_up, "w_down": w_down}


def slot_numbers(route_block):
    flat_ids = route_block.reshape(-1)
    labels = jnp.arange(EXPERTS, dtype=jnp.int32)
    onehot = (flat_ids[:, None] == labels[None, :]).astype(jnp.int32)
    before = jnp.cumsum(onehot, axis=0) - onehot
    return lax.optimization_barrier(jnp.sum(before * onehot, axis=1)).astype(jnp.int32).reshape(route_block.shape)

def attend_block(queries, keys_here, values, rates, state_in, gain_view):
    length_here = queries.shape[0]
    log_decay = -jnp.cumsum(rates, axis=1)
    last_log = log_decay[:, -1:]
    location_ordinals = jnp.arange(length_here)
    causal = (location_ordinals[:, None] >= location_ordinals[None, :])[None]
    spread = log_decay[:, :, None] - log_decay[:, None, :]
    weight = jnp.where(causal, jnp.exp(jnp.where(causal, spread, 0.0)), 0.0)
    scores = jnp.einsum('thd,shd->hts', queries.astype(jnp.float32), keys_here.astype(jnp.float32)) * weight
    weights_low = lax.optimization_barrier(scores.astype(jnp.bfloat16))
    inner_term = jnp.einsum('hts,shd->thd', weights_low.astype(jnp.float32), values.astype(jnp.float32))
    state_low = lax.optimization_barrier(state_in.astype(jnp.bfloat16))
    outer_term = jnp.einsum('thd,hde->the', queries.astype(jnp.float32), state_low.astype(jnp.float32))
    outer_term = outer_term * jnp.exp(log_decay).T[:, :, None]
    scaled_keys = (keys_here.astype(jnp.float32) * jnp.exp(last_log - log_decay).T[:, :, None]).astype(jnp.bfloat16)
    scaled_keys = lax.optimization_barrier(scaled_keys)
    local_state = jnp.einsum('thd,the->hde', scaled_keys.astype(jnp.float32), values.astype(jnp.float32))
    block_decay = jnp.exp(last_log[:, 0])
    combined = inner_term + outer_term
    normed = combined * lax.rsqrt(lax.optimization_barrier(jnp.mean(combined * combined, axis=-1, keepdims=True)) + 1e-06) * gain_view[None]
    return (normed.astype(jnp.bfloat16), block_decay, local_state)

def expert_layer(expert_rows, gate_pair, up_pair, down_pair):
    halves = []
    for owner_half in range(2):
        gate_act = jnp.dot(expert_rows, gate_pair[owner_half], preferred_element_type=jnp.float32)
        up_act = jnp.dot(expert_rows, up_pair[owner_half], preferred_element_type=jnp.float32)
        hidden = lax.optimization_barrier((jax.nn.silu(gate_act) * up_act).astype(jnp.bfloat16))
        pieces = hidden.reshape(-1, N_EXP, FFQ).astype(jnp.float32)
        down_pieces = down_pair[owner_half].reshape(N_EXP, FFQ, D).astype(jnp.float32)
        partial_value = lax.optimization_barrier(jnp.einsum('rxf,xfd->xrd', pieces, down_pieces).astype(jnp.bfloat16))
        quarter = lax.optimization_barrier(lax.optimization_barrier(jnp.sum(partial_value.astype(jnp.float32), axis=0)).astype(jnp.bfloat16))
        halves.append(quarter.astype(jnp.float32))
    return (halves[0] + halves[1]).astype(jnp.bfloat16)

def reference(query_heads, key_heads, value_heads, decay_rate, norm_gain, moe_input, route_ids, route_gates, w_gate, w_up, w_down):
    query_blocks = query_heads.reshape(N_SEQ, BLOCK, ATTENTION_COUNT, HD)
    key_blocks = key_heads.reshape(N_SEQ, BLOCK, ATTENTION_COUNT, HD)
    value_blocks = value_heads.reshape(N_SEQ, BLOCK, ATTENTION_COUNT, HD)
    rate_blocks = decay_rate.reshape(ATTENTION_COUNT, N_SEQ, BLOCK).transpose(1, 0, 2)
    gain_view = norm_gain.reshape(ATTENTION_COUNT, HD)

    def advance(state_now, items):
        queries, keys_here, values, rates = items
        normed, block_decay, local_state = attend_block(queries, keys_here, values, rates, state_now, gain_view)
        state_next = block_decay[:, None, None] * state_now + local_state
        return (state_next, normed)
    start_state = jnp.zeros((ATTENTION_COUNT, HD, HD), jnp.float32)
    _, attn_blocks = lax.scan(advance, start_state, (query_blocks, key_blocks, value_blocks, rate_blocks))
    attn_out = attn_blocks.reshape(TOKEN_SPAN, ATTENTION_COUNT * HD)
    device_count = N_SEQ * N_EXP
    id_blocks = route_ids.reshape(device_count, ROWS, 2)
    slots = jax.vmap(slot_numbers)(id_blocks)
    targets = id_blocks * CAP + slots
    token_blocks = moe_input.reshape(device_count, ROWS, D)

    def pack(items):
        target_block, token_block = items
        columns = jnp.arange(EXPERTS * CAP, dtype=jnp.int32)[:, None]
        selector = ((columns == target_block[None, :, 0]) | (columns == target_block[None, :, 1])).astype(jnp.bfloat16)
        return jnp.dot(selector, token_block, preferred_element_type=jnp.float32).astype(jnp.bfloat16)
    buffers = lax.map(pack, (targets, token_blocks))
    buffers = buffers.reshape(device_count, EXPERTS, CAP, D).transpose(1, 0, 2, 3).reshape(EXPERTS, device_count * CAP, D)

    def run_expert(items):
        return expert_layer(items[0], items[1], items[2], items[3])
    results = lax.map(run_expert, (buffers, w_gate.reshape(EXPERTS, 2, D, FFH), w_up.reshape(EXPERTS, 2, D, FFH), w_down.reshape(EXPERTS, 2, FFH, D)))
    flat_results = results.reshape(EXPERTS * device_count * CAP, D)
    owners = jnp.arange(device_count, dtype=jnp.int32)[:, None, None]
    index = ((id_blocks * device_count + owners) * CAP + slots).reshape(TOKEN_SPAN, 2).astype(jnp.int32)
    first_pick = jnp.take(flat_results, index[:, 0], axis=0).astype(jnp.float32)
    second_pick = jnp.take(flat_results, index[:, 1], axis=0).astype(jnp.float32)
    moe_out = (route_gates[:, 0:1] * first_pick + route_gates[:, 1:2] * second_pick).astype(jnp.bfloat16)
    return (attn_out, moe_out)
```

```python
import functools

import jax
import jax.numpy as jnp
from jax import lax
from jax.experimental import pallas as pl
from jax.experimental.pallas import tpu as pltpu
from jax.sharding import Mesh, PartitionSpec as P

HD = 128
MAIN = 16
TAIL = 2
FOLD = MAIN // TAIL
F32 = jnp.float32
BF16 = jnp.bfloat16
VMEM = pl.BlockSpec(memory_space=pltpu.VMEM)
SMEM = pl.BlockSpec(memory_space=pltpu.SMEM)
ANY = pl.BlockSpec(memory_space=pl.ANY)


def dot(a, b, dims=((1,), (0,))):
    return lax.dot_general(a, b, (dims, ((), ())), preferred_element_type=F32)


def iota(shape, dim):
    return lax.broadcasted_iota(jnp.int32, shape, dim)


def row_targets(ids, experts):
    rows = ids.shape[1]
    names = iota((experts, rows), 0)
    first = (names == ids[0:1]).astype(F32)
    second = (names == ids[1:2]).astype(F32)
    earlier = (iota((rows, rows), 0) < iota((rows, rows), 1)).astype(BF16)
    before = dot((first + second).astype(BF16), earlier)
    out = []
    for k, hot in enumerate((first, second)):
        slot = jnp.sum(hot * before, axis=0, keepdims=True).astype(jnp.int32)
        base = ids[k : k + 1] * MAIN
        main = jnp.where(slot < MAIN, base + slot, -1)
        tail = jnp.where(slot < MAIN, -1, base + (slot - MAIN) * FOLD)
        out.append((main, tail))
    return out


def pack_kernel(place_ref, ids_ref, x_ref, c0_ref, c1_ref, *, experts):
    rows, model = x_ref.shape
    ids = ids_ref[:, pl.ds(pl.multiple_of(place_ref[0] * rows, rows), rows)]
    (main0, tail0), (main1, tail1) = row_targets(ids, experts)
    row = iota((experts * MAIN, rows), 0)
    chosen = ((row == main0) | (row == main1)).astype(BF16)
    half = model // 2
    c0_ref[:, :half] = dot(chosen, x_ref[:, :half]).astype(BF16)
    c1_ref[:, :half] = dot(chosen, x_ref[:, half:]).astype(BF16)
    fold = row - row % FOLD
    folded = (fold == tail0) | (fold == tail1)
    width = model // FOLD
    total = jnp.zeros((experts * MAIN, width), F32)
    for q in range(FOLD):
        part = (folded & (row % FOLD == q)).astype(BF16)
        total = total + dot(part, x_ref[:, q * width : (q + 1) * width])
    total = total.astype(BF16)
    cut = c0_ref.shape[1] - half
    c0_ref[:, half:] = total[:, :cut]
    c1_ref[:, half:] = total[:, cut:]


def combine_kernel(place_ref, ids_ref, gates_ref, r0_ref, r1_ref, out_ref, *, experts):
    rows, model = out_ref.shape
    here = pl.ds(pl.multiple_of(place_ref[0] * rows, rows), rows)
    ids = ids_ref[:, here]
    gates = gates_ref[:, here]
    (main0, tail0), (main1, tail1) = row_targets(ids, experts)
    lines = [t.astype(F32) for t in (main0, tail0, main1, tail1)] + [gates]
    lines.append(jnp.zeros((rows - 6, rows), F32))
    turned = jnp.concatenate(lines, axis=0).T
    col = iota((rows, experts * MAIN), 1)
    half = model // 2
    cut = r0_ref.shape[1] - half
    width = model // FOLD
    picks = []
    for k in range(2):
        main = turned[:, 2 * k : 2 * k + 1].astype(jnp.int32)
        tail = turned[:, 2 * k + 1 : 2 * k + 2].astype(jnp.int32)
        chosen = (col == main).astype(BF16)
        folded = (col - col % FOLD) == tail
        parts = [dot(chosen, r0_ref[:, :half]), dot(chosen, r1_ref[:, :half])]
        pieces = []
        for q in range(FOLD):
            part = (folded & (col % FOLD == q)).astype(BF16)
            pieces.append(
                jnp.concatenate(
                    [dot(part, r0_ref[:, half:]), dot(part, r1_ref[:, half:])], axis=1
                )
            )
        picks.append(jnp.concatenate(parts, axis=1) + jnp.concatenate(pieces, axis=1))
    out_ref[...] = (turned[:, 4:5] * picks[0] + turned[:, 5:6] * picks[1]).astype(BF16)


def ffn_kernel(*refs, blocks, sources):
    xs = refs[: 2 * blocks]
    weights = refs[2 * blocks : 2 * blocks + 6]
    ys = refs[2 * blocks + 6 : 4 * blocks + 6]
    held = refs[4 * blocks + 6 : 4 * blocks + 12]
    x_all, sems = refs[4 * blocks + 12 :]
    copies = [
        pltpu.make_async_copy(w, h, sems.at[i]) for i, (w, h) in enumerate(zip(weights, held))
    ]
    for copy in copies:
        copy.start()
    rows = sources * MAIN
    short = sources * TAIL
    model = x_all.shape[1]
    half = model // 2
    cut = xs[0].shape[1] - half
    width = model // FOLD
    row, col = iota((short, rows), 0), iota((short, rows), 1)
    match = [(col == row * FOLD + q).astype(BF16) for q in range(FOLD)]
    back_row, back_col = iota((rows, short), 0), iota((rows, short), 1)
    back = [(back_row == back_col * FOLD + q).astype(BF16) for q in range(FOLD)]
    for b in range(blocks):
        lo, hi = xs[2 * b], xs[2 * b + 1]
        x_all[b * rows : (b + 1) * rows, :half] = lo[:, :half]
        x_all[b * rows : (b + 1) * rows, half:] = hi[:, :half]
        at = blocks * rows + b * short
        for q in range(FOLD):
            x_all[at : at + short, q * width : q * width + cut] = dot(
                match[q], lo[:, half:]
            ).astype(BF16)
            x_all[at : at + short, q * width + cut : (q + 1) * width] = dot(
                match[q], hi[:, half:]
            ).astype(BF16)
    total = None
    for p in range(2):
        copies[3 * p].wait()
        gate = dot(x_all[...], held[3 * p][...])
        copies[3 * p + 1].wait()
        up = dot(x_all[...], held[3 * p + 1][...])
        hidden = (gate * (1.0 / (1.0 + jnp.exp(-gate))) * up).astype(BF16)
        copies[3 * p + 2].wait()
        part = dot(hidden, held[3 * p + 2][...])
        total = part if total is None else total + part
    total = total.astype(BF16)
    for b in range(blocks):
        lo, hi = ys[2 * b], ys[2 * b + 1]
        lo[:, :half] = total[b * rows : (b + 1) * rows, :half]
        hi[:, :half] = total[b * rows : (b + 1) * rows, half:]
        at = blocks * rows + b * short
        tail = total[at : at + short]
        folded = jnp.zeros((rows, width), F32)
        for q in range(FOLD):
            folded = folded + dot(back[q], tail[:, q * width : (q + 1) * width])
        folded = folded.astype(BF16)
        lo[:, half:] = folded[:, :cut]
        hi[:, half:] = folded[:, cut:]


def run_experts(pairs, weights):
    blocks = len(pairs)
    flat = [x for pair in pairs for x in pair]
    rows = flat[0].shape[0]
    sources = rows // MAIN
    model, hidden = weights[0].shape
    total_rows = blocks * (rows + sources * TAIL)
    outs = pl.pallas_call(
        functools.partial(ffn_kernel, blocks=blocks, sources=sources),
        out_shape=[jax.ShapeDtypeStruct(x.shape, BF16) for x in flat],
        in_specs=[VMEM] * len(flat) + [ANY] * 6,
        out_specs=[VMEM] * len(flat),
        scratch_shapes=[pltpu.VMEM(w.shape, BF16) for w in weights]
        + [pltpu.VMEM((total_rows, model), BF16), pltpu.SemaphoreType.DMA((6,))],
        compiler_params=pltpu.CompilerParams(vmem_limit_bytes=56 * 1024 * 1024),
        cost_estimate=pl.CostEstimate(
            flops=12 * total_rows * model * hidden,
            bytes_accessed=12 * model * hidden + 8 * total_rows * model,
            transcendentals=2 * total_rows * hidden,
        ),
        name="experts",
    )(*flat, *weights)
    return [(outs[2 * b], outs[2 * b + 1]) for b in range(blocks)]


def log_decays(rates):
    span = rates.shape[1]
    high = rates.astype(BF16)
    rest = rates - high.astype(F32)
    mid = rest.astype(BF16)
    low = (rest - mid.astype(F32)).astype(BF16)
    earlier = (iota((span, span), 0) <= iota((span, span), 1)).astype(BF16)
    later = (iota((span, span), 0) >= iota((span, span), 1)).astype(BF16)
    by_row = dot(high, earlier) + (dot(mid, earlier) + dot(low, earlier))
    turn = ((1,), (1,))
    by_col = dot(later, high, turn) + (dot(later, mid, turn) + dot(later, low, turn))
    return -by_row, -by_col


def head_column(by_col, head):
    return jnp.sum(jnp.where(iota(by_col.shape, 1) == head, by_col, 0.0), axis=1, keepdims=True)


def state_kernel(rates_ref, k_ref, v_ref, out_ref, by_row, by_col):
    head = pl.program_id(0)

    @pl.when(head == 0)
    def _():
        by_row[...], by_col[...] = log_decays(rates_ref[...])

    here = head_column(by_col[...], head)
    last = here[-1:, :]
    scaled = (k_ref[...].astype(F32) * jnp.exp(last - here)).astype(BF16)
    state = dot(scaled, v_ref[...], ((0,), (0,))).astype(BF16)
    half = HD // 2
    decay = jnp.exp(last)
    high = decay.astype(BF16).astype(F32)
    mid = (decay - high).astype(BF16).astype(F32)
    low = decay - high - mid
    lead = iota((16, HD), 0)
    extra = jnp.where(lead == 0, high, jnp.where(lead == 1, mid, jnp.where(lead == 2, low, 0.0)))
    for i in range(2):
        out_ref[i, :half, :] = state[i * half : (i + 1) * half]
        out_ref[i, half:, :] = extra.astype(BF16)


def scan_kernel(in_ref, out_ref):
    count, rows, _ = out_ref.shape
    state = jnp.zeros(out_ref.shape[1:], F32)
    for b in range(count):
        out_ref[b] = state.astype(BF16)
        extra = in_ref[b, rows:, :].astype(F32)
        decay = extra[0:1] + extra[1:2] + extra[2:3]
        state = decay * state + in_ref[b, :rows, :].astype(F32)


def attend_kernel(rates_ref, gain_ref, q_ref, k_ref, v_ref, state_ref, out_ref, by_row, by_col):
    head = pl.program_id(0)

    @pl.when(head == 0)
    def _():
        by_row[...], by_col[...] = log_decays(rates_ref[...])

    span = q_ref.shape[0]
    column = head_column(by_col[...], head)
    line = by_row[pl.ds(head, 1), :]
    step = span // 2
    for start in range(0, span, step):
        end = start + step
        queries = q_ref[start:end, :]
        here = column[start:end]
        spread = here - line[:, :end]
        causal = start + iota((step, end), 0) >= iota((step, end), 1)
        weight = jnp.where(causal, jnp.exp(jnp.where(causal, spread, 0.0)), 0.0)
        scores = dot(queries, k_ref[:end, :], ((1,), (1,))) * weight
        inner = dot(scores.astype(BF16), v_ref[:end, :])
        outer = dot(queries, state_ref[0]) * jnp.exp(here)
        both = inner + outer
        scale = lax.rsqrt(jnp.mean(both * both, axis=1, keepdims=True) + 1e-06)
        out_ref[start:end, :] = (both * scale * gain_ref[...]).astype(BF16)


def head_spec(span):
    return pl.BlockSpec((span, HD), lambda h: (0, h))


def decay_scratch(heads, span):
    return [pltpu.VMEM((heads, span), F32), pltpu.VMEM((span, heads), F32)]


def local_states(rates, keys, values):
    heads, span = rates.shape
    return pl.pallas_call(
        state_kernel,
        grid=(heads,),
        out_shape=jax.ShapeDtypeStruct((2 * heads, HD // 2 + 16, HD), BF16),
        in_specs=[pl.BlockSpec((heads, span), lambda h: (0, 0))] + [head_spec(span)] * 2,
        out_specs=pl.BlockSpec((2, HD // 2 + 16, HD), lambda h: (h, 0, 0)),
        scratch_shapes=decay_scratch(heads, span),
        cost_estimate=pl.CostEstimate(
            flops=2 * heads * span * HD * HD, bytes_accessed=4 * heads * span * HD, transcendentals=0
        ),
        name="local_states",
    )(rates, keys, values)


def attend(rates, gain, queries, keys, values, states):
    heads, span = rates.shape
    return pl.pallas_call(
        attend_kernel,
        grid=(heads,),
        out_shape=jax.ShapeDtypeStruct(queries.shape, BF16),
        in_specs=[
            pl.BlockSpec((heads, span), lambda h: (0, 0)),
            pl.BlockSpec((1, HD), lambda h: (0, h)),
        ]
        + [head_spec(span)] * 3
        + [pl.BlockSpec((1, HD, HD), lambda h: (h, 0, 0))],
        out_specs=head_spec(span),
        scratch_shapes=decay_scratch(heads, span),
        cost_estimate=pl.CostEstimate(
            flops=4 * heads * span * span * HD,
            bytes_accessed=8 * heads * span * HD,
            transcendentals=heads * span * span,
        ),
        name="attend",
    )(rates, gain, queries, keys, values, states)


def local(
    query_heads,
    key_heads,
    value_heads,
    decay_rate,
    norm_gain,
    moe_input,
    route_ids,
    route_gates,
    w_gate,
    w_up,
    w_down,
):
    rows, model = moe_input.shape
    experts = lax.axis_size("chip")
    ring = lax.axis_size("exp")
    place = lax.axis_index("exp").astype(jnp.int32).reshape(1)
    ids = route_ids.T
    gates = route_gates.T

    own_weights = [w_gate[0], w_up[0], w_down[0]]
    other_weights = [lax.ppermute(w, "core", [(0, 1), (1, 0)]) for w in own_weights]
    weights = own_weights + other_weights

    half = model // 2
    fold = model // FOLD
    widths = (half + fold // 3, half + fold - fold // 3)
    packed = pl.pallas_call(
        functools.partial(pack_kernel, experts=experts),
        out_shape=[jax.ShapeDtypeStruct((experts * MAIN, w), BF16) for w in widths],
        in_specs=[SMEM, VMEM, VMEM],
        out_specs=[VMEM, VMEM],
        name="pack",
    )(place, ids, moe_input)

    def swap_rows(x):
        blocks = x.reshape(experts, MAIN, x.shape[1])
        return lax.all_to_all(blocks, "chip", 0, 0, tiled=True).reshape(x.shape)

    up_ring = [(i, (i + 1) % ring) for i in range(ring)]
    down_ring = [(i, (i - 1) % ring) for i in range(ring)]

    def send_up(x):
        return lax.ppermute(x, "exp", up_ring)

    def send_down(x):
        return lax.ppermute(x, "exp", down_ring)

    own = [swap_rows(x) for x in packed]
    below = [send_up(x) for x in own]
    above = [send_down(x) for x in own]
    across = [send_up(below[0]), send_down(above[1])]

    states = local_states(decay_rate, key_heads, value_heads)
    arrived = lax.all_to_all(states, ("chip", "core"), 0, 0, tiled=True)
    count = arrived.shape[0]
    entering = pl.pallas_call(
        scan_kernel,
        out_shape=jax.ShapeDtypeStruct((count, HD // 2, HD), BF16),
        in_specs=[VMEM],
        out_specs=VMEM,
        name="scan",
    )(arrived)
    entering = lax.all_to_all(entering, ("chip", "core"), 0, 0, tiled=True)
    attn_out = attend(
        decay_rate,
        norm_gain.reshape(1, -1),
        query_heads,
        key_heads,
        value_heads,
        entering.reshape(-1, HD, HD),
    )

    (y_own,) = run_experts([own], weights)
    y_below, y_above = run_experts([below, above], weights)
    (y_across,) = run_experts([across], weights)

    def add(*terms):
        return sum(t.astype(F32) for t in terms).astype(BF16)

    go_up = [add(y_above[0], send_up(y_across[0])), y_above[1]]
    go_down = [y_below[0], add(y_below[1], send_down(y_across[1]))]
    sums = [add(o, send_up(u), send_down(d)) for o, u, d in zip(y_own, go_up, go_down)]
    returned = [swap_rows(x) for x in sums]
    moe_out = pl.pallas_call(
        functools.partial(combine_kernel, experts=experts),
        out_shape=jax.ShapeDtypeStruct((rows, model), BF16),
        in_specs=[SMEM] + [VMEM] * 4,
        out_specs=VMEM,
        name="combine",
    )(place, ids, gates, *returned)
    return (attn_out, moe_out)


def solution(mesh):
    seq, exp = mesh.devices.shape
    split = Mesh(mesh.devices.reshape(seq // 2, 2, exp), ("chip", "core", "exp"))
    seq = ("chip", "core")
    everything = ("chip", "core", "exp")
    placed = (
        P(seq, "exp"),
        P(seq, "exp"),
        P(seq, "exp"),
        P("exp", seq),
        P("exp"),
        P(everything, None),
        P(seq, None),
        P(seq, None),
        P(seq, None, "exp"),
        P(seq, None, "exp"),
        P(seq, "exp", None),
    )
    return jax.shard_map(
        local,
        mesh=split,
        in_specs=placed,
        out_specs=(P(seq, "exp"), P(everything, None)),
        check_vma=False,
    )
```

```python
import functools

import jax
import jax.numpy as jnp
from jax import lax
from jax.experimental import pallas as pl
from jax.experimental.pallas import tpu as pltpu
from jax.sharding import Mesh, PartitionSpec as P

HD = 128
CHUNKS = 2
MAIN = 8
F32 = jnp.float32
BF16 = jnp.bfloat16
VMEM = pl.BlockSpec(memory_space=pltpu.VMEM)
SMEM = pl.BlockSpec(memory_space=pltpu.SMEM)
ANY = pl.BlockSpec(memory_space=pl.ANY)


def after(value, *others):
    return lax.optimization_barrier((value, others))[0]


def dot(a, b, dims=((1,), (0,))):
    return lax.dot_general(a, b, (dims, ((), ())), preferred_element_type=F32)


def iota(shape, dim):
    return lax.broadcasted_iota(jnp.int32, shape, dim)


def row_targets(ids, experts):
    rows = ids.shape[1]
    names = iota((experts, rows), 0)
    first = (names == ids[0:1]).astype(F32)
    second = (names == ids[1:2]).astype(F32)
    earlier = (iota((rows, rows), 0) < iota((rows, rows), 1)).astype(BF16)
    before = dot((first + second).astype(BF16), earlier)
    span = experts * (MAIN + 1)
    out = []
    for k, hot in enumerate((first, second)):
        slot = jnp.sum(hot * before, axis=0, keepdims=True).astype(jnp.int32)
        here = ids[k : k + 1]
        target = experts * MAIN + here + (slot - CHUNKS * MAIN) * span
        for c in range(CHUNKS):
            inside = slot - c * MAIN
            target = jnp.where(
                (inside >= 0) & (inside < MAIN), c * span + here * MAIN + inside, target
            )
        out.append(target)
    return out


def unfold(folded):
    rows = folded.shape[0]
    count = rows // MAIN
    row, col = iota((rows, rows), 0), iota((rows, rows), 1)
    flat = dot((col == row % count * MAIN + row // count).astype(BF16), folded).astype(BF16)
    return jnp.concatenate([flat[q * count : (q + 1) * count] for q in range(MAIN)], axis=1)


def refold(whole):
    count, model = whole.shape
    rows, width = count * MAIN, model // MAIN
    flat = jnp.concatenate([whole[:, q * width : (q + 1) * width] for q in range(MAIN)], axis=0)
    row, col = iota((rows, rows), 0), iota((rows, rows), 1)
    return dot((col == row % MAIN * count + row // MAIN).astype(BF16), flat).astype(BF16)


def pack_kernel(place_ref, ids_ref, x_ref, *out_refs, experts):
    rows, model = x_ref.shape
    ids = ids_ref[:, pl.ds(pl.multiple_of(place_ref[0] * rows, rows), rows)]
    first, second = row_targets(ids, experts)
    span = experts * (MAIN + 1)
    row = iota((CHUNKS * span, rows), 0)
    chosen = ((row == first) | (row == second)).astype(BF16)
    picked = dot(chosen, x_ref[...]).astype(BF16)
    for c, out_ref in enumerate(out_refs):
        out_ref[:, :model] = picked[c * span : c * span + experts * MAIN]
        out_ref[:, model:] = refold(picked[c * span + experts * MAIN : (c + 1) * span])


def combine_kernel(place_ref, ids_ref, gates_ref, *refs, experts):
    in_refs, out_ref = refs[:CHUNKS], refs[CHUNKS]
    rows, model = out_ref.shape
    here = pl.ds(pl.multiple_of(place_ref[0] * rows, rows), rows)
    first, second = row_targets(ids_ref[:, here], experts)
    lines = [first.astype(F32), second.astype(F32), gates_ref[:, here]]
    lines.append(jnp.zeros((rows - 4, rows), F32))
    turned = jnp.concatenate(lines, axis=0).T
    col = iota((rows, CHUNKS * experts * (MAIN + 1)), 1)
    chosen = [(col == turned[:, k : k + 1].astype(jnp.int32)).astype(BF16) for k in range(2)]
    chosen = jnp.concatenate(chosen, axis=0)
    held = [part for r in in_refs for part in (r[:, :model], unfold(r[:, model:]))]
    picks = dot(chosen, jnp.concatenate(held, axis=0))
    out_ref[...] = (turned[:, 2:3] * picks[:rows] + turned[:, 3:4] * picks[rows:]).astype(BF16)


def ffn_kernel(*refs, blocks, sources):
    xs = refs[:blocks]
    own = refs[blocks : blocks + 6 : 2]
    other = refs[blocks + 1 : blocks + 6 : 2]
    ys = refs[blocks + 6 : 2 * blocks + 6]
    gate_w, up_w, down_w, x_all, hid, y_all, tails, sems = refs[2 * blocks + 6 :]
    part = own[0].shape[0]
    first = part - part % 256
    rows = sources * MAIN
    model = x_all.shape[1]
    half = model // 2
    width = model // MAIN
    issued = []

    def begin(src, dst):
        copy = pltpu.make_async_copy(src, dst, sems.at[len(issued)])
        copy.start()
        issued.append(copy)
        return copy

    def piece(held, own_ref, other_ref, stage):
        if stage == 0:
            return [begin(own_ref.at[pl.ds(0, first)], held.at[pl.ds(0, first)])]
        rest = part - first
        return [
            begin(own_ref.at[pl.ds(first, rest)], held.at[pl.ds(first, rest)]),
            begin(other_ref, held.at[pl.ds(part, part)]),
        ]

    loads = []
    for b, x in enumerate(xs):
        here = pl.ds(b * rows, rows)
        loads.append(begin(x.at[:, pl.ds(model, width)], tails.at[here]))
        loads.append(begin(x.at[:, pl.ds(0, model)], x_all.at[here]))
    stages = []
    for stage in range(2):
        stages.append(
            (
                piece(gate_w, own[0], other[0], stage),
                piece(up_w, own[1], other[1], stage),
            )
        )
    down = [
        begin(own[2], down_w.at[pl.ds(0, part)]),
        begin(other[2], down_w.at[pl.ds(part, part)]),
    ]

    for copy in loads:
        copy.wait()
    for b in range(blocks):
        at = blocks * rows + b * sources
        x_all[at : at + sources, :] = unfold(tails[b * rows : (b + 1) * rows, :])
    turn = ((1,), (1,))
    for stage, (lo, hi) in enumerate(((0, first), (first, 2 * part))):
        for copy in stages[stage][0]:
            copy.wait()
        gate = dot(x_all[...], gate_w[lo:hi, :], turn)
        for copy in stages[stage][1]:
            copy.wait()
        up = dot(x_all[...], up_w[lo:hi, :], turn)
        hid[:, lo:hi] = (gate * (1.0 / (1.0 + jnp.exp(-gate))) * up).astype(BF16)
    for copy in down:
        copy.wait()
    stores = []
    for c in range(2):
        y_all[:, c * half : (c + 1) * half] = dot(
            hid[...], down_w[:, c * half : (c + 1) * half]
        ).astype(BF16)
        columns = pl.ds(c * half, half)
        for b, y in enumerate(ys):
            stores.append(begin(y_all.at[pl.ds(b * rows, rows), columns], y.at[:, columns]))
    for b, y in enumerate(ys):
        at = blocks * rows + b * sources
        tails[b * rows : (b + 1) * rows, :] = refold(y_all[at : at + sources, :])
        stores.append(begin(tails.at[pl.ds(b * rows, rows)], y.at[:, pl.ds(model, width)]))
    for copy in stores:
        copy.wait()


def run_experts(xs, weights, sources):
    hidden, model = weights[0].shape
    rows = sources * MAIN
    blocks = len(xs)
    total_rows = blocks * (rows + sources)
    return pl.pallas_call(
        functools.partial(ffn_kernel, blocks=blocks, sources=sources),
        out_shape=[jax.ShapeDtypeStruct(x.shape, BF16) for x in xs],
        in_specs=[ANY] * (blocks + 6),
        out_specs=[ANY] * blocks,
        scratch_shapes=[pltpu.VMEM((2 * hidden, model), BF16)] * 3
        + [
            pltpu.VMEM((total_rows, model), BF16),
            pltpu.VMEM((total_rows, 2 * hidden), BF16),
            pltpu.VMEM((total_rows, model), BF16),
            pltpu.VMEM((blocks * rows, model // MAIN), BF16),
            pltpu.SemaphoreType.DMA((5 * blocks + 8,)),
        ],
        compiler_params=pltpu.CompilerParams(vmem_limit_bytes=56 * 1024 * 1024),
        cost_estimate=pl.CostEstimate(
            flops=12 * total_rows * model * hidden,
            bytes_accessed=12 * model * hidden + 8 * total_rows * model,
            transcendentals=2 * total_rows * hidden,
        ),
        name="experts",
    )(*xs, *weights)


def log_decays(rates):
    span = rates.shape[1]
    high = rates.astype(BF16)
    rest = rates - high.astype(F32)
    mid = rest.astype(BF16)
    low = (rest - mid.astype(F32)).astype(BF16)
    earlier = (iota((span, span), 0) <= iota((span, span), 1)).astype(BF16)
    later = (iota((span, span), 0) >= iota((span, span), 1)).astype(BF16)
    by_row = dot(high, earlier) + (dot(mid, earlier) + dot(low, earlier))
    turn = ((1,), (1,))
    by_col = dot(later, high, turn) + (dot(later, mid, turn) + dot(later, low, turn))
    return -by_row, -by_col


def state_kernel(rates_ref, k_ref, v_ref, out_ref, scales, ends):
    step = pl.program_id(0)
    group = out_ref.shape[0] // 2

    @pl.when(step == 0)
    def _():
        _, by_col = log_decays(rates_ref[...])
        last = by_col[-1:, :]
        scale = jnp.exp(last - by_col)
        end = jnp.broadcast_to(jnp.exp(last), (8, last.shape[1]))
        for g in range(scales.shape[0]):
            scales[g] = scale[:, g * group : (g + 1) * group]
            ends[g] = end[:, g * group : (g + 1) * group]

    half = HD // 2
    lead = iota((16, HD), 0)
    scale = scales[step]
    end = ends[step]
    for i in range(group):
        columns = slice(i * HD, (i + 1) * HD)
        scaled = (k_ref[:, columns].astype(F32) * scale[:, i : i + 1]).astype(BF16)
        state = dot(scaled, v_ref[:, columns], ((0,), (0,))).astype(BF16)
        decay = end[0:1, i : i + 1]
        high = decay.astype(BF16).astype(F32)
        mid = (decay - high).astype(BF16).astype(F32)
        low = decay - high - mid
        extra = jnp.where(
            lead == 0, high, jnp.where(lead == 1, mid, jnp.where(lead == 2, low, 0.0))
        ).astype(BF16)
        for j in range(2):
            out_ref[2 * i + j, :half, :] = state[j * half : (j + 1) * half]
            out_ref[2 * i + j, half:, :] = extra


def scan_kernel(in_ref, out_ref):
    count, rows, _ = out_ref.shape
    state = jnp.zeros(out_ref.shape[1:], F32)
    for b in range(count):
        out_ref[b] = state.astype(BF16)
        extra = in_ref[b, rows:, :].astype(F32)
        decay = extra[0:1] + extra[1:2] + extra[2:3]
        state = decay * state + in_ref[b, :rows, :].astype(F32)


def inner_kernel(rates_ref, q_ref, k_ref, v_ref, out_ref, growth_ref, by_row, columns):
    step = pl.program_id(0)
    group = columns.shape[2]

    @pl.when(step == 0)
    def _():
        by_row[...], by_col = log_decays(rates_ref[...])
        growth_ref[...] = jnp.exp(by_col)
        for g in range(columns.shape[0]):
            columns[g] = by_col[:, g * group : (g + 1) * group]

    span = q_ref.shape[0]
    size = span // 2
    here = columns[step]
    causal = iota((size, size), 0) >= iota((size, size), 1)
    for i in range(group):
        wide = slice(i * HD, (i + 1) * HD)
        line = by_row[pl.ds(step * group + i, 1), :]
        for start in range(0, span, size):
            end = start + size
            column = here[start:end, i : i + 1]
            queries = q_ref[start:end, wide]
            weight = jnp.exp(jnp.minimum(column - line[:, start:end], 0.0))
            scores = dot(queries, k_ref[start:end, wide], ((1,), (1,))) * weight
            scores = jnp.where(causal, scores, 0.0).astype(BF16)
            total = dot(scores, v_ref[start:end, wide])
            if start:
                weight = jnp.exp(jnp.minimum(column - line[:, :start], 0.0))
                scores = dot(queries, k_ref[:start, wide], ((1,), (1,))) * weight
                total = total + dot(scores.astype(BF16), v_ref[:start, wide])
            out_ref[start:end, wide] = total


def outer_kernel(growth_ref, gain_ref, q_ref, inner_ref, state_ref, out_ref, columns):
    step = pl.program_id(0)
    group = columns.shape[2]

    @pl.when(step == 0)
    def _():
        for g in range(columns.shape[0]):
            columns[g] = growth_ref[:, g * group : (g + 1) * group]

    here = columns[step]
    for i in range(group):
        wide = slice(i * HD, (i + 1) * HD)
        outer = dot(q_ref[:, wide], state_ref[i]) * here[:, i : i + 1]
        both = inner_ref[:, wide] + outer
        scale = lax.rsqrt(jnp.mean(both * both, axis=1, keepdims=True) + 1e-06)
        out_ref[:, wide] = (both * scale * gain_ref[:, wide]).astype(BF16)


GROUP = 4


def wide_spec(span):
    return pl.BlockSpec((span, GROUP * HD), lambda g: (0, g))


def whole_spec(*shape):
    return pl.BlockSpec(shape, lambda g: (0, 0))


def local_states(rates, keys, values):
    heads, span = rates.shape
    group = GROUP
    wide = wide_spec(span)
    return pl.pallas_call(
        state_kernel,
        grid=(heads // group,),
        out_shape=jax.ShapeDtypeStruct((2 * heads, HD // 2 + 16, HD), BF16),
        in_specs=[pl.BlockSpec((heads, span), lambda g: (0, 0)), wide, wide],
        out_specs=pl.BlockSpec((2 * group, HD // 2 + 16, HD), lambda g: (g, 0, 0)),
        scratch_shapes=[
            pltpu.VMEM((heads // group, span, group), F32),
            pltpu.VMEM((heads // group, 8, group), F32),
        ],
        cost_estimate=pl.CostEstimate(
            flops=2 * heads * span * HD * HD, bytes_accessed=4 * heads * span * HD, transcendentals=0
        ),
        name="local_states",
    )(rates, keys, values)


def inner_terms(rates, queries, keys, values):
    heads, span = rates.shape
    wide = wide_spec(span)
    return pl.pallas_call(
        inner_kernel,
        grid=(heads // GROUP,),
        out_shape=[
            jax.ShapeDtypeStruct(queries.shape, F32),
            jax.ShapeDtypeStruct((span, heads), F32),
        ],
        in_specs=[whole_spec(heads, span), wide, wide, wide],
        out_specs=[wide, whole_spec(span, heads)],
        scratch_shapes=[
            pltpu.VMEM((heads, span), F32),
            pltpu.VMEM((heads // GROUP, span, GROUP), F32),
        ],
        cost_estimate=pl.CostEstimate(
            flops=3 * heads * span * span * HD,
            bytes_accessed=10 * heads * span * HD,
            transcendentals=heads * span * span,
        ),
        name="inner_terms",
    )(rates, queries, keys, values)


def attend(growth, gain, queries, inner, states):
    span, heads = growth.shape
    wide = wide_spec(span)
    return pl.pallas_call(
        outer_kernel,
        grid=(heads // GROUP,),
        out_shape=jax.ShapeDtypeStruct(queries.shape, BF16),
        in_specs=[
            whole_spec(span, heads),
            pl.BlockSpec((1, GROUP * HD), lambda g: (0, g)),
            wide,
            wide,
            pl.BlockSpec((GROUP, HD, HD), lambda g: (g, 0, 0)),
        ],
        out_specs=wide,
        scratch_shapes=[pltpu.VMEM((heads // GROUP, span, GROUP), F32)],
        cost_estimate=pl.CostEstimate(
            flops=2 * heads * span * HD * HD, bytes_accessed=8 * heads * span * HD, transcendentals=0
        ),
        name="attend",
    )(growth, gain, queries, inner, states)


def local(
    query_heads,
    key_heads,
    value_heads,
    decay_rate,
    norm_gain,
    moe_input,
    route_ids,
    route_gates,
    w_gate,
    w_up,
    w_down,
):
    rows, model = moe_input.shape
    experts = lax.axis_size("chip")
    ring = lax.axis_size("exp")
    place = lax.axis_index("exp").astype(jnp.int32).reshape(1)
    ids = route_ids.T
    gates = route_gates.T

    own_weights = [w_gate[0].T, w_up[0].T, w_down[0]]
    other_weights = [lax.ppermute(w, "core", [(0, 1), (1, 0)]) for w in own_weights]
    weights = [w for pair in zip(own_weights, other_weights) for w in pair]

    chunk = jax.ShapeDtypeStruct((experts * MAIN, model + model // MAIN), BF16)
    packed = pl.pallas_call(
        functools.partial(pack_kernel, experts=experts),
        out_shape=[chunk] * CHUNKS,
        in_specs=[SMEM, VMEM, VMEM],
        out_specs=[VMEM] * CHUNKS,
        name="pack",
    )(place, ids, moe_input)

    def swap_rows(x):
        blocks = x.reshape(experts, MAIN, x.shape[1])
        return lax.all_to_all(blocks, "chip", 0, 0, tiled=True).reshape(x.shape)

    up_ring = [(i, (i + 1) % ring) for i in range(ring)]
    down_ring = [(i, (i - 1) % ring) for i in range(ring)]

    def send_up(x):
        return lax.ppermute(x, "exp", up_ring)

    def send_down(x):
        return lax.ppermute(x, "exp", down_ring)

    inner, growth = inner_terms(decay_rate, query_heads, key_heads, value_heads)
    own0 = swap_rows(packed[0])
    ready0 = after(own0, weights, inner)
    below0 = send_up(ready0)
    above0 = send_down(ready0)
    own1 = swap_rows(after(packed[1], own0))
    states = local_states(after(decay_rate, own0), key_heads, value_heads)
    ready1 = after(own1, below0, above0, states)
    above1 = send_down(ready1)
    across0 = send_up(below0)
    below1 = send_up(after(ready1, across0))
    arrived = lax.all_to_all(after(states, own1), ("chip", "core"), 0, 0, tiled=True)
    y_below0, y_above0 = run_experts([below0, above0], weights, experts)
    count = arrived.shape[0]
    entering = pl.pallas_call(
        scan_kernel,
        out_shape=jax.ShapeDtypeStruct((count, HD // 2, HD), BF16),
        in_specs=[VMEM],
        out_specs=VMEM,
        name="scan",
    )(after(arrived, y_below0))
    across0 = after(across0, above1, entering)
    entering = lax.all_to_all(after(entering, across0), ("chip", "core"), 0, 0, tiled=True)
    across1 = send_down(above1)
    y_across0, y_own0 = run_experts([across0, own0], weights, experts)
    (y_across1,) = run_experts([after(across1, y_across0, below1)], weights, experts)

    def add(*terms):
        return sum(t.astype(F32) for t in terms).astype(BF16)

    y_back0 = send_down(after(y_below0, y_across0))
    go_up0 = add(y_above0, after(send_up(y_across0), y_across1))
    y_below1, y_above1, y_own1 = run_experts(
        [after(below1, y_across1, go_up0, entering), above1, own1], weights, experts
    )
    from_below1 = send_up(y_above1)
    go_down1 = add(y_below1, send_down(y_across1))
    sums0 = add(y_own0, send_up(go_up0), y_back0)
    sums1 = add(y_own1, from_below1, send_down(go_down1))
    attn_out = attend(
        growth,
        norm_gain.reshape(1, -1),
        query_heads,
        after(inner, sums0),
        entering.reshape(-1, HD, HD),
    )
    returned = [swap_rows(sums0), swap_rows(sums1)]
    moe_out = pl.pallas_call(
        functools.partial(combine_kernel, experts=experts),
        out_shape=jax.ShapeDtypeStruct((rows, model), BF16),
        in_specs=[SMEM] + [VMEM] * (2 + CHUNKS),
        out_specs=VMEM,
        name="combine",
    )(place, ids, gates, *returned)
    return (attn_out, moe_out)


def solution(mesh):
    seq, exp = mesh.devices.shape
    split = Mesh(mesh.devices.reshape(seq // 2, 2, exp), ("chip", "core", "exp"))
    seq = ("chip", "core")
    everything = ("chip", "core", "exp")
    placed = (
        P(seq, "exp"),
        P(seq, "exp"),
        P(seq, "exp"),
        P("exp", seq),
        P("exp"),
        P(everything, None),
        P(seq, None),
        P(seq, None),
        P(seq, None, "exp"),
        P(seq, None, "exp"),
        P(seq, "exp", None),
    )
    return jax.shard_map(
        local,
        mesh=split,
        in_specs=placed,
        out_specs=(P(seq, "exp"), P(everything, None)),
        check_vma=False,
    )
```

```python
import functools

import jax
import jax.numpy as jnp
from jax import lax
from jax.experimental import pallas as pl
from jax.experimental.pallas import tpu as pltpu
from jax.sharding import Mesh, PartitionSpec as P

HD = 128
CHUNKS = 2
MAIN = 8
F32 = jnp.float32
BF16 = jnp.bfloat16
VMEM = pl.BlockSpec(memory_space=pltpu.VMEM)
SMEM = pl.BlockSpec(memory_space=pltpu.SMEM)
ANY = pl.BlockSpec(memory_space=pl.ANY)


def after(value, *others):
    return lax.optimization_barrier((value, others))[0]


def dot(a, b, dims=((1,), (0,))):
    return lax.dot_general(a, b, (dims, ((), ())), preferred_element_type=F32)


def iota(shape, dim):
    return lax.broadcasted_iota(jnp.int32, shape, dim)


def row_targets(ids, experts):
    rows = ids.shape[1]
    names = iota((experts, rows), 0)
    first = (names == ids[0:1]).astype(F32)
    second = (names == ids[1:2]).astype(F32)
    earlier = (iota((rows, rows), 0) < iota((rows, rows), 1)).astype(BF16)
    before = dot((first + second).astype(BF16), earlier)
    span = experts * (MAIN + 1)
    out = []
    for k, hot in enumerate((first, second)):
        slot = jnp.sum(hot * before, axis=0, keepdims=True).astype(jnp.int32)
        here = ids[k : k + 1]
        target = experts * MAIN + here + (slot - CHUNKS * MAIN) * span
        for c in range(CHUNKS):
            inside = slot - c * MAIN
            target = jnp.where(
                (inside >= 0) & (inside < MAIN), c * span + here * MAIN + inside, target
            )
        out.append(target)
    return out


def unfold(folded):
    rows = folded.shape[0]
    count = rows // MAIN
    row, col = iota((rows, rows), 0), iota((rows, rows), 1)
    flat = dot((col == row % count * MAIN + row // count).astype(BF16), folded).astype(BF16)
    return jnp.concatenate([flat[q * count : (q + 1) * count] for q in range(MAIN)], axis=1)


def refold(whole):
    count, model = whole.shape
    rows, width = count * MAIN, model // MAIN
    flat = jnp.concatenate([whole[:, q * width : (q + 1) * width] for q in range(MAIN)], axis=0)
    row, col = iota((rows, rows), 0), iota((rows, rows), 1)
    return dot((col == row % MAIN * count + row // MAIN).astype(BF16), flat).astype(BF16)


def pack_kernel(place_ref, ids_ref, x_ref, out_ref, *, experts, chunk):
    rows, model = x_ref.shape
    ids = ids_ref[:, pl.ds(pl.multiple_of(place_ref[0] * rows, rows), rows)]
    first, second = row_targets(ids, experts)
    span = experts * (MAIN + 1)
    row = iota((span, rows), 0) + chunk * span
    chosen = ((row == first) | (row == second)).astype(BF16)
    picked = dot(chosen, x_ref[...]).astype(BF16)
    out_ref[:, :model] = picked[: experts * MAIN]
    out_ref[:, model:] = refold(picked[experts * MAIN :])


def combine_kernel(place_ref, ids_ref, gates_ref, *refs, experts):
    in_refs, out_ref, held, tails, sems = refs[:CHUNKS], *refs[CHUNKS:]
    rows, model = out_ref.shape
    whole = experts * MAIN
    span = whole + experts
    copies = []
    for c, in_ref in enumerate(in_refs):
        pairs = (
            (in_ref.at[:, pl.ds(model, model // MAIN)], tails.at[c]),
            (in_ref.at[:, pl.ds(0, model)], held.at[pl.ds(c * span, whole)]),
        )
        for j, (src, dst) in enumerate(pairs):
            copies.append(pltpu.make_async_copy(src, dst, sems.at[2 * c + j]))
            copies[-1].start()
    here = pl.ds(pl.multiple_of(place_ref[0] * rows, rows), rows)
    first, second = row_targets(ids_ref[:, here], experts)
    lines = [first.astype(F32), second.astype(F32), gates_ref[:, here]]
    lines.append(jnp.zeros((rows - 4, rows), F32))
    turned = jnp.concatenate(lines, axis=0).T
    col = iota((rows, CHUNKS * span), 1)
    chosen = [(col == turned[:, k : k + 1].astype(jnp.int32)).astype(BF16) for k in range(2)]
    chosen = jnp.concatenate(chosen, axis=0)
    for c in range(CHUNKS):
        copies[2 * c].wait()
        held[c * span + whole : (c + 1) * span, :] = unfold(tails[c])
        copies[2 * c + 1].wait()
    picks = dot(chosen, held[...])
    out_ref[...] = (turned[:, 2:3] * picks[:rows] + turned[:, 3:4] * picks[rows:]).astype(BF16)


def ffn_kernel(*refs, blocks, sources):
    xs = refs[:blocks]
    own = refs[blocks : blocks + 6 : 2]
    other = refs[blocks + 1 : blocks + 6 : 2]
    ys = refs[blocks + 6 : 2 * blocks + 6]
    gate_w, up_w, down_w, x_all, hid, y_all, tails, sems = refs[2 * blocks + 6 :]
    part = own[0].shape[0]
    first = part - part % 256
    rows = sources * MAIN
    model = x_all.shape[1]
    half = model // 2
    width = model // MAIN
    issued = []

    def begin(src, dst):
        copy = pltpu.make_async_copy(src, dst, sems.at[len(issued)])
        copy.start()
        issued.append(copy)
        return copy

    def piece(held, own_ref, other_ref, stage):
        if stage == 0:
            return [begin(own_ref.at[pl.ds(0, first)], held.at[pl.ds(0, first)])]
        rest = part - first
        return [
            begin(own_ref.at[pl.ds(first, rest)], held.at[pl.ds(first, rest)]),
            begin(other_ref, held.at[pl.ds(part, part)]),
        ]

    loads = []
    for b, x in enumerate(xs):
        here = pl.ds(b * rows, rows)
        loads.append(begin(x.at[:, pl.ds(model, width)], tails.at[here]))
        loads.append(begin(x.at[:, pl.ds(0, model)], x_all.at[here]))
    stages = []
    for stage in range(2):
        stages.append(
            (
                piece(gate_w, own[0], other[0], stage),
                piece(up_w, own[1], other[1], stage),
            )
        )
    down = [
        begin(own[2], down_w.at[pl.ds(0, part)]),
        begin(other[2], down_w.at[pl.ds(part, part)]),
    ]

    for copy in loads:
        copy.wait()
    for b in range(blocks):
        at = blocks * rows + b * sources
        x_all[at : at + sources, :] = unfold(tails[b * rows : (b + 1) * rows, :])
    turn = ((1,), (1,))
    for stage, (lo, hi) in enumerate(((0, first), (first, 2 * part))):
        for copy in stages[stage][0]:
            copy.wait()
        gate = dot(x_all[...], gate_w[lo:hi, :], turn)
        for copy in stages[stage][1]:
            copy.wait()
        up = dot(x_all[...], up_w[lo:hi, :], turn)
        hid[:, lo:hi] = (gate * (1.0 / (1.0 + jnp.exp(-gate))) * up).astype(BF16)
    for copy in down:
        copy.wait()
    stores = []
    for c in range(2):
        y_all[:, c * half : (c + 1) * half] = dot(
            hid[...], down_w[:, c * half : (c + 1) * half]
        ).astype(BF16)
        columns = pl.ds(c * half, half)
        for b, y in enumerate(ys):
            stores.append(begin(y_all.at[pl.ds(b * rows, rows), columns], y.at[:, columns]))
    for b, y in enumerate(ys):
        at = blocks * rows + b * sources
        tails[b * rows : (b + 1) * rows, :] = refold(y_all[at : at + sources, :])
        stores.append(begin(tails.at[pl.ds(b * rows, rows)], y.at[:, pl.ds(model, width)]))
    for copy in stores:
        copy.wait()


def run_experts(xs, weights, sources):
    hidden, model = weights[0].shape
    rows = sources * MAIN
    blocks = len(xs)
    total_rows = blocks * (rows + sources)
    return pl.pallas_call(
        functools.partial(ffn_kernel, blocks=blocks, sources=sources),
        out_shape=[jax.ShapeDtypeStruct(x.shape, BF16) for x in xs],
        in_specs=[ANY] * (blocks + 6),
        out_specs=[ANY] * blocks,
        scratch_shapes=[pltpu.VMEM((2 * hidden, model), BF16)] * 3
        + [
            pltpu.VMEM((total_rows, model), BF16),
            pltpu.VMEM((total_rows, 2 * hidden), BF16),
            pltpu.VMEM((total_rows, model), BF16),
            pltpu.VMEM((blocks * rows, model // MAIN), BF16),
            pltpu.SemaphoreType.DMA((5 * blocks + 8,)),
        ],
        compiler_params=pltpu.CompilerParams(vmem_limit_bytes=56 * 1024 * 1024),
        cost_estimate=pl.CostEstimate(
            flops=12 * total_rows * model * hidden,
            bytes_accessed=12 * model * hidden + 8 * total_rows * model,
            transcendentals=2 * total_rows * hidden,
        ),
        name="experts",
    )(*xs, *weights)


def log_decays(rates):
    span = rates.shape[1]
    high = rates.astype(BF16)
    rest = rates - high.astype(F32)
    mid = rest.astype(BF16)
    low = (rest - mid.astype(F32)).astype(BF16)
    earlier = (iota((span, span), 0) <= iota((span, span), 1)).astype(BF16)
    later = (iota((span, span), 0) >= iota((span, span), 1)).astype(BF16)
    by_row = dot(high, earlier) + (dot(mid, earlier) + dot(low, earlier))
    turn = ((1,), (1,))
    by_col = dot(later, high, turn) + (dot(later, mid, turn) + dot(later, low, turn))
    return -by_row, -by_col


def state_kernel(rates_ref, k_ref, v_ref, out_ref, scales, ends):
    step = pl.program_id(0)
    group = out_ref.shape[0] // 2

    @pl.when(step == 0)
    def _():
        _, by_col = log_decays(rates_ref[...])
        last = by_col[-1:, :]
        scale = jnp.exp(last - by_col)
        end = jnp.broadcast_to(jnp.exp(last), (8, last.shape[1]))
        for g in range(scales.shape[0]):
            scales[g] = scale[:, g * group : (g + 1) * group]
            ends[g] = end[:, g * group : (g + 1) * group]

    half = HD // 2
    lead = iota((16, HD), 0)
    scale = scales[step]
    end = ends[step]
    for i in range(group):
        columns = slice(i * HD, (i + 1) * HD)
        scaled = (k_ref[:, columns].astype(F32) * scale[:, i : i + 1]).astype(BF16)
        state = dot(scaled, v_ref[:, columns], ((0,), (0,))).astype(BF16)
        decay = end[0:1, i : i + 1]
        high = decay.astype(BF16).astype(F32)
        mid = (decay - high).astype(BF16).astype(F32)
        low = decay - high - mid
        extra = jnp.where(
            lead == 0, high, jnp.where(lead == 1, mid, jnp.where(lead == 2, low, 0.0))
        ).astype(BF16)
        for j in range(2):
            out_ref[2 * i + j, :half, :] = state[j * half : (j + 1) * half]
            out_ref[2 * i + j, half:, :] = extra


def scan_kernel(in_ref, out_ref):
    count, rows, _ = out_ref.shape
    state = jnp.zeros(out_ref.shape[1:], F32)
    for b in range(count):
        out_ref[b] = state.astype(BF16)
        extra = in_ref[b, rows:, :].astype(F32)
        decay = extra[0:1] + extra[1:2] + extra[2:3]
        state = decay * state + in_ref[b, :rows, :].astype(F32)


def inner_kernel(rates_ref, q_ref, k_ref, v_ref, out_ref, growth_ref, by_row, columns):
    step = pl.program_id(0)
    group = columns.shape[2]

    @pl.when(step == 0)
    def _():
        by_row[...], by_col = log_decays(rates_ref[...])
        growth_ref[...] = jnp.exp(by_col)
        for g in range(columns.shape[0]):
            columns[g] = by_col[:, g * group : (g + 1) * group]

    span = q_ref.shape[0]
    size = span // 2
    here = columns[step]
    causal = iota((size, size), 0) >= iota((size, size), 1)
    for i in range(group):
        wide = slice(i * HD, (i + 1) * HD)
        line = by_row[pl.ds(step * group + i, 1), :]
        for start in range(0, span, size):
            end = start + size
            column = here[start:end, i : i + 1]
            queries = q_ref[start:end, wide]
            weight = jnp.exp(jnp.minimum(column - line[:, start:end], 0.0))
            scores = dot(queries, k_ref[start:end, wide], ((1,), (1,))) * weight
            scores = jnp.where(causal, scores, 0.0).astype(BF16)
            total = dot(scores, v_ref[start:end, wide])
            if start:
                weight = jnp.exp(jnp.minimum(column - line[:, :start], 0.0))
                scores = dot(queries, k_ref[:start, wide], ((1,), (1,))) * weight
                total = total + dot(scores.astype(BF16), v_ref[:start, wide])
            out_ref[start:end, wide] = total


def outer_kernel(growth_ref, gain_ref, q_ref, inner_ref, state_ref, out_ref, columns):
    step = pl.program_id(0)
    group = columns.shape[2]

    @pl.when(step == 0)
    def _():
        for g in range(columns.shape[0]):
            columns[g] = growth_ref[:, g * group : (g + 1) * group]

    here = columns[step]
    for i in range(group):
        wide = slice(i * HD, (i + 1) * HD)
        outer = dot(q_ref[:, wide], state_ref[i]) * here[:, i : i + 1]
        both = inner_ref[:, wide] + outer
        scale = lax.rsqrt(jnp.mean(both * both, axis=1, keepdims=True) + 1e-06)
        out_ref[:, wide] = (both * scale * gain_ref[:, wide]).astype(BF16)


GROUP = 4


def wide_spec(span):
    return pl.BlockSpec((span, GROUP * HD), lambda g: (0, g))


def whole_spec(*shape):
    return pl.BlockSpec(shape, lambda g: (0, 0))


def local_states(rates, keys, values):
    heads, span = rates.shape
    group = GROUP
    wide = wide_spec(span)
    return pl.pallas_call(
        state_kernel,
        grid=(heads // group,),
        out_shape=jax.ShapeDtypeStruct((2 * heads, HD // 2 + 16, HD), BF16),
        in_specs=[pl.BlockSpec((heads, span), lambda g: (0, 0)), wide, wide],
        out_specs=pl.BlockSpec((2 * group, HD // 2 + 16, HD), lambda g: (g, 0, 0)),
        scratch_shapes=[
            pltpu.VMEM((heads // group, span, group), F32),
            pltpu.VMEM((heads // group, 8, group), F32),
        ],
        cost_estimate=pl.CostEstimate(
            flops=2 * heads * span * HD * HD, bytes_accessed=4 * heads * span * HD, transcendentals=0
        ),
        name="local_states",
    )(rates, keys, values)


def inner_terms(rates, queries, keys, values):
    heads, span = rates.shape
    wide = wide_spec(span)
    return pl.pallas_call(
        inner_kernel,
        grid=(heads // GROUP,),
        out_shape=[
            jax.ShapeDtypeStruct(queries.shape, F32),
            jax.ShapeDtypeStruct((span, heads), F32),
        ],
        in_specs=[whole_spec(heads, span), wide, wide, wide],
        out_specs=[wide, whole_spec(span, heads)],
        scratch_shapes=[
            pltpu.VMEM((heads, span), F32),
            pltpu.VMEM((heads // GROUP, span, GROUP), F32),
        ],
        cost_estimate=pl.CostEstimate(
            flops=3 * heads * span * span * HD,
            bytes_accessed=10 * heads * span * HD,
            transcendentals=heads * span * span,
        ),
        name="inner_terms",
    )(rates, queries, keys, values)


def attend(growth, gain, queries, inner, states):
    span, heads = growth.shape
    wide = wide_spec(span)
    return pl.pallas_call(
        outer_kernel,
        grid=(heads // GROUP,),
        out_shape=jax.ShapeDtypeStruct(queries.shape, BF16),
        in_specs=[
            whole_spec(span, heads),
            pl.BlockSpec((1, GROUP * HD), lambda g: (0, g)),
            wide,
            wide,
            pl.BlockSpec((GROUP, HD, HD), lambda g: (g, 0, 0)),
        ],
        out_specs=wide,
        scratch_shapes=[pltpu.VMEM((heads // GROUP, span, GROUP), F32)],
        cost_estimate=pl.CostEstimate(
            flops=2 * heads * span * HD * HD, bytes_accessed=28 * heads * span * HD, transcendentals=0
        ),
        name="attend",
    )(growth, gain, queries, inner, states)


def local(
    query_heads,
    key_heads,
    value_heads,
    decay_rate,
    norm_gain,
    moe_input,
    route_ids,
    route_gates,
    w_gate,
    w_up,
    w_down,
):
    rows, model = moe_input.shape
    experts = lax.axis_size("chip")
    ring = lax.axis_size("exp")
    place = lax.axis_index("exp").astype(jnp.int32).reshape(1)
    ids = route_ids.T
    gates = route_gates.T

    own_weights = [w_gate[0].T, w_up[0].T, w_down[0]]
    other_weights = [lax.ppermute(w, "core", [(0, 1), (1, 0)]) for w in own_weights]
    weights = [w for pair in zip(own_weights, other_weights) for w in pair]

    chunk = jax.ShapeDtypeStruct((experts * MAIN, model + model // MAIN), BF16)
    packed = [
        pl.pallas_call(
            functools.partial(pack_kernel, experts=experts, chunk=c),
            out_shape=chunk,
            in_specs=[SMEM, VMEM, VMEM],
            out_specs=VMEM,
            cost_estimate=pl.CostEstimate(
                flops=2 * chunk.size * rows, bytes_accessed=4 * chunk.size, transcendentals=0
            ),
            name="pack",
        )(place, ids, moe_input)
        for c in range(CHUNKS)
    ]

    def swap_rows(x):
        blocks = x.reshape(experts, MAIN, x.shape[1])
        return lax.all_to_all(blocks, "chip", 0, 0, tiled=True).reshape(x.shape)

    up_ring = [(i, (i + 1) % ring) for i in range(ring)]
    down_ring = [(i, (i - 1) % ring) for i in range(ring)]

    def send_up(x):
        return lax.ppermute(x, "exp", up_ring)

    def send_down(x):
        return lax.ppermute(x, "exp", down_ring)

    inner, growth = inner_terms(decay_rate, query_heads, key_heads, value_heads)
    own0 = swap_rows(packed[0])
    ready0 = after(own0, weights, inner, packed[1])
    below0 = send_up(ready0)
    above0 = send_down(ready0)
    own1 = swap_rows(after(packed[1], own0))
    states = local_states(after(decay_rate, own0), key_heads, value_heads)
    ready1 = after(own1, below0, above0, states)
    above1 = send_down(ready1)
    across0 = send_up(below0)
    below1 = send_up(after(ready1, across0))
    arrived = lax.all_to_all(after(states, own1), ("chip", "core"), 0, 0, tiled=True)
    y_below0, y_above0 = run_experts([below0, above0], weights, experts)
    count = arrived.shape[0]
    entering = pl.pallas_call(
        scan_kernel,
        out_shape=jax.ShapeDtypeStruct((count, HD // 2, HD), BF16),
        in_specs=[VMEM],
        out_specs=VMEM,
        name="scan",
    )(after(arrived, y_below0))
    across0 = after(across0, above1, entering)
    entering = lax.all_to_all(after(entering, across0), ("chip", "core"), 0, 0, tiled=True)
    across1 = send_down(above1)
    y_across0, y_own0 = run_experts([across0, own0], weights, experts)
    (y_across1,) = run_experts([after(across1, y_across0, below1)], weights, experts)

    def add(*terms):
        return sum(t.astype(F32) for t in terms).astype(BF16)

    y_back0 = send_down(after(y_below0, y_across0))
    go_up0 = add(y_above0, after(send_up(y_across0), y_across1))
    y_below1, y_above1, y_own1 = run_experts(
        [after(below1, y_across1, go_up0, entering), above1, own1], weights, experts
    )
    from_below1 = send_up(y_above1)
    go_down1 = add(y_below1, send_down(y_across1))
    sums0 = add(y_own0, send_up(go_up0), y_back0)
    attn_out = attend(
        growth,
        norm_gain.reshape(1, -1),
        query_heads,
        after(inner, sums0),
        entering.reshape(-1, HD, HD),
    )
    sums1 = add(after(y_own1, attn_out), from_below1, send_down(go_down1))
    returned = [swap_rows(sums0), swap_rows(sums1)]
    moe_out = pl.pallas_call(
        functools.partial(combine_kernel, experts=experts),
        out_shape=jax.ShapeDtypeStruct((rows, model), BF16),
        in_specs=[SMEM, VMEM, VMEM] + [ANY] * CHUNKS,
        out_specs=VMEM,
        scratch_shapes=[
            pltpu.VMEM((CHUNKS * experts * (MAIN + 1), model), BF16),
            pltpu.VMEM((CHUNKS, experts * MAIN, model // MAIN), BF16),
            pltpu.SemaphoreType.DMA((2 * CHUNKS,)),
        ],
        name="combine",
    )(place, ids, gates, *returned)
    return (attn_out, moe_out)


def solution(mesh):
    seq, exp = mesh.devices.shape
    split = Mesh(mesh.devices.reshape(seq // 2, 2, exp), ("chip", "core", "exp"))
    seq = ("chip", "core")
    everything = ("chip", "core", "exp")
    placed = (
        P(seq, "exp"),
        P(seq, "exp"),
        P(seq, "exp"),
        P("exp", seq),
        P("exp"),
        P(everything, None),
        P(seq, None),
        P(seq, None),
        P(seq, None, "exp"),
        P(seq, None, "exp"),
        P(seq, "exp", None),
    )
    return jax.shard_map(
        local,
        mesh=split,
        in_specs=placed,
        out_specs=(P(seq, "exp"), P(everything, None)),
        check_vma=False,
    )
```
